32 devices in a mesh: grp: 2 (over x), seq: 16 (over z, y, core).
Axes of the slice: x: 2, y: 2, z: 4, core: 2. Of those that a mesh axis runs over, the one named last changes fastest.
Arguments:
- raw_queries: bfloat16 [4096, 4096], P(('grp', 'seq')), parts along dimension 0, as said below
- beacon_queries: bfloat16 [128, 4096], P(('grp', 'seq')), parts along dimension 0, may hold values from -6 to 6
- raw_keys: bfloat16 [4096, 512], P(('grp', 'seq')), parts along dimension 0, as said below
- raw_values: bfloat16 [4096, 512], P(('grp', 'seq')), parts along dimension 0, may hold values from -6 to 6
- beacon_keys: bfloat16 [128, 512], P(('grp', 'seq')), parts along dimension 0, may hold values from -6 to 6
- beacon_values: bfloat16 [128, 512], P(('grp', 'seq')), parts along dimension 0, may hold values from -6 to 6
- raw_cotangent: bfloat16 [4096, 4096], P(('grp', 'seq')), parts along dimension 0, may hold values from -6 to 6
- beacon_cotangent: bfloat16 [128, 4096], P(('grp', 'seq')), parts along dimension 0, may hold values from -6 to 6
- slot_span: int32 [32], P('grp'), parts along dimension 0, may hold values from 0 to 15, each once
- beacon_counts: int32 [32], P('grp'), parts along dimension 0, may hold values from 1 to 4, as said below
- first_span: int32 [32], P('grp'), parts along dimension 0, may hold values from 0 to 15, as said below
Outputs:
- raw_query_grad: bfloat16 [4096, 4096], P(('grp', 'seq')), parts along dimension 0
- beacon_query_grad: bfloat16 [128, 4096], P(('grp', 'seq')), parts along dimension 0
- raw_key_grad: bfloat16 [4096, 512], P(('grp', 'seq')), parts along dimension 0
- raw_value_grad: bfloat16 [4096, 512], P(('grp', 'seq')), parts along dimension 0
- beacon_key_grad: bfloat16 [128, 512], P(('grp', 'seq')), parts along dimension 0
- beacon_value_grad: bfloat16 [128, 512], P(('grp', 'seq')), parts along dimension 0
The draws below stay inside these ranges and needn't reach their ends.
There are 2 independent parts, one for each index of `grp`. The reference program is written for one: setup_inputs(seed, part) draws one part's arguments, and reference() takes and returns one part's arrays. A program takes and returns all parts, laid end to end along the dimension named above; each array names one. Nothing has to cross between parts.
Inputs may be any that keep to these rules, and one draw needn't show every extreme that they name: `raw_queries`: queries and keys lie within -6 to 6. `raw_keys`: keys lie within -6 to 6. `beacon_counts`: some span has exactly 4 live beacons and some span exactly one. first_span[c] <= c, it never falls along c, first_span[0] is 0, where first_span[c] differs from first_span[c-1] it equals c, and the last span begins a document of its own.
All inputs are finite; a program needn't handle non-finite values.
Results may differ from the reference program's by a relative error of at most 0.0065.
Values may be sent and summed in bfloat16 or wider, within the bound.
A program may use at most 64 MiB of HBM per device.

```python
import jax
import jax.numpy as jnp
from jax import lax

HEADS = 32
KV_HEADS = 4
HEAD_DIM = 128
SPAN = 128
BEACONS = 4
SPANS = 16
TOKENS = 2048
BEACON_ROWS = 64


def draw_raw_queries(key, part):
    key = jax.random.fold_in(key, 11)
    drawn = jnp.clip(jax.random.normal(key, (TOKENS, HEADS * HEAD_DIM), jnp.float32), -6.0, 6.0)
    return drawn.astype(jnp.bfloat16)


def draw_raw_keys(key, part):
    key = jax.random.fold_in(key, 12)
    drawn = jnp.clip(jax.random.normal(key, (TOKENS, KV_HEADS * HEAD_DIM), jnp.float32), -6.0, 6.0)
    return drawn.astype(jnp.bfloat16)


def draw_beacon_counts(key, part):
    key = jax.random.fold_in(key, 21)
    count_key, place_key = jax.random.split(key)
    drawn = jax.random.randint(count_key, (SPANS,), 1, BEACONS + 1, dtype=jnp.int32)
    fullest = jax.random.randint(place_key, (), 0, SPANS, dtype=jnp.int32)
    emptiest = (fullest + 1) % SPANS
    span_ids = jnp.arange(SPANS, dtype=jnp.int32)
    drawn = jnp.where(span_ids == emptiest, 1, drawn)
    return jnp.where(span_ids == fullest, BEACONS, drawn).astype(jnp.int32)


def draw_first_span(key, part):
    key = jax.random.fold_in(key, 31)
    first_key, second_key = jax.random.split(key)
    span_ids = jnp.arange(SPANS, dtype=jnp.int32)
    first_break = jax.random.randint(first_key, (), 1, SPANS - 1, dtype=jnp.int32)
    second_break = jax.random.randint(second_key, (), 1, SPANS - 1, dtype=jnp.int32)
    breaks = (span_ids == 0) | (span_ids == SPANS - 1) | (span_ids == first_break) | (span_ids == second_break)
    starts = jnp.where(breaks, span_ids, 0).astype(jnp.int32)
    return lax.cummax(starts, axis=0).astype(jnp.int32)


def block_levels(key, shape, cuts, low, high):
    level, own = 1.0, jax.random.fold_in(key, 6)
    for dim, shards_of in cuts:
        draws = jnp.exp(jax.random.uniform(jax.random.fold_in(own, dim), (shards_of,), jnp.float32, low / len(cuts), high / len(cuts)))
        level = level * jnp.repeat(draws, shape[dim] // shards_of).reshape([-1 if axis == dim else 1 for axis in range(len(shape))])
    return level


def centred(rng, shape, width, reach, shards=(), held_as=jnp.bfloat16):
    values = width * jax.random.normal(rng, shape, jnp.float32)
    if shards:
        values = values * block_levels(rng, shape, shards, -0.22, 0.18)
    return jnp.clip(values, -reach, reach).astype(held_as)


def setup_inputs(seed: int = 0, part: int = 0) -> dict:
    keys = jax.random.split(jax.random.key(seed), 12)
    part_keys = jax.random.split(jax.random.fold_in(keys[11], part), 12)
    return {
        "raw_queries": draw_raw_queries(jax.random.fold_in(jax.random.fold_in(keys[11], part), 71), part),
        "beacon_queries": centred(part_keys[1], (BEACON_ROWS, HEADS * HEAD_DIM), 1.0, 6.0, ((0, 16),)),
        "raw_keys": draw_raw_keys(jax.random.fold_in(jax.random.fold_in(keys[11], part), 71), part),
        "raw_values": centred(part_keys[3], (TOKENS, KV_HEADS * HEAD_DIM), 1.0, 6.0, ((0, 16),)),
        "beacon_keys": centred(part_keys[4], (BEACON_ROWS, KV_HEADS * HEAD_DIM), 1.0, 6.0, ((0, 16),)),
        "beacon_values": centred(part_keys[5], (BEACON_ROWS, KV_HEADS * HEAD_DIM), 1.0, 6.0, ((0, 16),)),
        "raw_cotangent": centred(part_keys[6], (TOKENS, HEADS * HEAD_DIM), 1.0, 6.0, ((0, 16),)),
        "beacon_cotangent": centred(part_keys[7], (BEACON_ROWS, HEADS * HEAD_DIM), 1.0, 6.0, ((0, 16),)),
        "slot_span": jax.random.permutation(part_keys[8], SPANS).astype(jnp.int32),
        "beacon_counts": draw_beacon_counts(jax.random.fold_in(jax.random.fold_in(keys[11], part), 71), part),
        "first_span": draw_first_span(jax.random.fold_in(jax.random.fold_in(keys[11], part), 71), part),
    }


def product(form, left_side, right_side):
    return jnp.einsum(form, left_side.astype(jnp.float32), right_side.astype(jnp.float32), precision=lax.Precision.HIGHEST)


def lookup(lookup_table, positions):
    width_count = lookup_table.shape[0]
    hits = positions[:, None] == jnp.arange(width_count)[None, :]
    return jnp.sum(jnp.where(hits, lookup_table[None, :], 0), axis=1)


def select_entry(entries, slot_index):
    return jnp.sum(jnp.where(jnp.arange(entries.shape[0]) == slot_index, entries, 0))


def visible(slot_span, beacon_counts, first_span, slot_index):
    span_count = slot_span.shape[0]
    slot_counts = lookup(beacon_counts, slot_span)
    slot_first = lookup(first_span, slot_span)
    own_span = select_entry(slot_span, slot_index)
    own_first = select_entry(slot_first, slot_index)
    own_count = select_entry(slot_counts, slot_index)
    key_span = jnp.repeat(slot_span, BEACONS)
    key_slot = jnp.repeat(jnp.arange(span_count), BEACONS)
    key_beacon = jnp.tile(jnp.arange(BEACONS), span_count)
    key_live = key_beacon < jnp.repeat(slot_counts, BEACONS)
    earlier = (own_first <= key_span) & (key_span < own_span) & key_live
    raw_ids = jnp.arange(SPAN)
    beacon_ids = jnp.arange(BEACONS)
    raw_part = jnp.concatenate([jnp.broadcast_to(earlier[None, :], (SPAN, earlier.shape[0])), raw_ids[None, :] <= raw_ids[:, None]], axis=1)
    own_beacons = (key_slot[None, :] == slot_index) & (key_beacon[None, :] <= beacon_ids[:, None]) & key_live[None, :]
    beacon_part = jnp.concatenate([earlier[None, :] | own_beacons, jnp.ones((BEACONS, SPAN), bool)], axis=1)
    allowed = jnp.concatenate([raw_part, beacon_part], axis=0)
    live_rows = jnp.concatenate([jnp.ones((SPAN,), bool), beacon_ids < own_count])
    return allowed, live_rows


def slot_pass(queries, cotangents, key_rows, value_rows, allowed):
    score_scale = HEAD_DIM ** -0.5
    row_count = queries.shape[0]
    group_size = HEADS // KV_HEADS
    query_parts, key_parts, value_parts = [], [], []
    for kv_head in range(KV_HEADS):
        low = kv_head * group_size * HEAD_DIM
        high = (kv_head + 1) * group_size * HEAD_DIM
        q_head = queries[:, low:high].reshape(row_count, group_size, HEAD_DIM)
        g_head = cotangents[:, low:high].reshape(row_count, group_size, HEAD_DIM)
        k_head = key_rows[:, kv_head * HEAD_DIM:(kv_head + 1) * HEAD_DIM]
        v_head = value_rows[:, kv_head * HEAD_DIM:(kv_head + 1) * HEAD_DIM]
        scores = product("mgd,nd->gmn", q_head, k_head) * score_scale
        scores = jnp.where(allowed[None], scores, -1e30)
        row_max = jnp.max(scores, axis=-1, keepdims=True)
        row_total = jnp.sum(jnp.exp(scores - row_max), axis=-1, keepdims=True)
        logsum = row_max + jnp.log(row_total)
        attention = jnp.exp(scores - logsum)
        attention_grad = product("mgd,nd->gmn", g_head, v_head)
        row_delta = jnp.sum(attention * attention_grad, axis=-1, keepdims=True)
        score_grad = lax.optimization_barrier((attention * (attention_grad - row_delta) * score_scale).astype(jnp.bfloat16))
        attention_low = lax.optimization_barrier(attention.astype(jnp.bfloat16))
        query_parts.append(product("gmn,nd->mgd", score_grad, k_head).reshape(row_count, group_size * HEAD_DIM))
        key_parts.append(product("gmn,mgd->nd", score_grad, q_head))
        value_parts.append(product("gmn,mgd->nd", attention_low, g_head))
    return (jnp.concatenate(query_parts, axis=1).astype(jnp.bfloat16),
            jnp.concatenate(key_parts, axis=1), jnp.concatenate(value_parts, axis=1))


def reference(raw_queries, beacon_queries, raw_keys, raw_values, beacon_keys, beacon_values,
              raw_cotangent, beacon_cotangent, slot_span, beacon_counts, first_span):
    span_count = slot_span.shape[0]
    beacon_total = span_count * BEACONS
    kv_width = KV_HEADS * HEAD_DIM

    def slot_step(beacon_term, slot_index):
        raw_start = (slot_index * SPAN).astype(jnp.int32)
        beacon_start = (slot_index * BEACONS).astype(jnp.int32)
        queries = jnp.concatenate([lax.dynamic_slice_in_dim(raw_queries, raw_start, SPAN, 0),
                                   lax.dynamic_slice_in_dim(beacon_queries, beacon_start, BEACONS, 0)], axis=0)
        cotangents = jnp.concatenate([lax.dynamic_slice_in_dim(raw_cotangent, raw_start, SPAN, 0),
                                      lax.dynamic_slice_in_dim(beacon_cotangent, beacon_start, BEACONS, 0)], axis=0)
        allowed, live_rows = visible(slot_span, beacon_counts, first_span, slot_index)
        cotangents = jnp.where(live_rows[:, None], cotangents, jnp.zeros_like(cotangents))
        key_rows = jnp.concatenate([beacon_keys, lax.dynamic_slice_in_dim(raw_keys, raw_start, SPAN, 0)], axis=0)
        value_rows = jnp.concatenate([beacon_values, lax.dynamic_slice_in_dim(raw_values, raw_start, SPAN, 0)], axis=0)
        query_grad, key_grad, value_grad = slot_pass(queries, cotangents, key_rows, value_rows, allowed)
        beacon_term = beacon_term + jnp.concatenate([key_grad[:beacon_total], value_grad[:beacon_total]], axis=1)
        return beacon_term, (query_grad[:SPAN], query_grad[SPAN:],
                             key_grad[beacon_total:].astype(jnp.bfloat16), value_grad[beacon_total:].astype(jnp.bfloat16))

    start_term = jnp.zeros((beacon_total, 2 * kv_width), jnp.float32)
    beacon_term, stacked = lax.scan(slot_step, start_term, jnp.arange(span_count, dtype=jnp.int32))
    raw_query_grad = stacked[0].reshape(span_count * SPAN, HEADS * HEAD_DIM)
    beacon_query_grad = stacked[1].reshape(beacon_total, HEADS * HEAD_DIM)
    raw_key_grad = stacked[2].reshape(span_count * SPAN, kv_width)
    raw_value_grad = stacked[3].reshape(span_count * SPAN, kv_width)
    beacon_key_grad = beacon_term[:, :kv_width].astype(jnp.bfloat16)
    beacon_value_grad = beacon_term[:, kv_width:].astype(jnp.bfloat16)
    return (raw_query_grad, beacon_query_grad, raw_key_grad, raw_value_grad, beacon_key_grad, beacon_value_grad)
```

```python
import functools

import jax
import jax.numpy as jnp
from jax import lax
from jax.experimental import pallas as pl
from jax.experimental.pallas import tpu as pltpu
from jax.sharding import PartitionSpec as P

HEADS = 32
KV = 4
D = 128
SPAN = 128
B = 4
GROUP = HEADS // KV
CHUNK = 256
WIDE = GROUP * SPAN
SCALE = D ** (-0.5)
EXP2 = SCALE * 1.4426950408889634
LOW = -1e30
F32 = jnp.float32
BF16 = jnp.bfloat16
MESH = pl.DeviceIdType.MESH


def nt(a, b):
    return lax.dot_general(a, b, (((1,), (1,)), ((), ())), preferred_element_type=F32)


def nn(a, b):
    return lax.dot_general(a, b, (((1,), (0,)), ((), ())), preferred_element_type=F32)


def tn(a, b):
    return lax.dot_general(a, b, (((0,), (0,)), ((), ())), preferred_element_type=F32)


def each(n, body):
    if n <= 16:
        for d in range(1, n):
            body(d)
    else:
        lax.fori_loop(1, n, lambda d, c: (body(d), c)[1], 0)


def stack_heads(ref, kv, first, count):
    low = (kv * GROUP + first) * D
    return jnp.concatenate([ref[:, low + i * D : low + (i + 1) * D] for i in range(count)], axis=0)


def kernel(
    n,
    rq, bq, rk, rv, bk, bv, rg, bg, ss, bc, fs,
    rq_out, bq_out, rk_out, rv_out, bk_out, bv_out,
    q, g, k, v, bqs, bgs, bks, bvs,
    qx, gx, msg, gat, kb, vb,
    p_r, dp_r, p_x, dp_x, stat,
    a_all, ds_all, sbuf, rbuf, oq, obq, ok, ov, obk, obv,
    local_sem, out_sem, ag_send, ag_recv, rs_send, rs_recv,
):
    me = lax.axis_index("seq")
    rows = n * B

    small = [
        pltpu.make_async_copy(a, b, local_sem.at[i])
        for i, (a, b) in enumerate([(bk, bks), (bv, bvs), (rk, k), (rv, v), (bq, bqs), (bg, bgs)])
    ]
    for c in small:
        c.start()
    large = []
    for kv in range(KV):
        cols = pl.ds(kv * WIDE, WIDE)
        cq = pltpu.make_async_copy(rq.at[:, cols], q.at[:, cols], local_sem.at[6 + 2 * kv])
        cg = pltpu.make_async_copy(rg.at[:, cols], g.at[:, cols], local_sem.at[7 + 2 * kv])
        cq.start()
        cg.start()
        large.append((cq, cg))

    barrier = pltpu.get_barrier_semaphore()

    def greet(d):
        pl.semaphore_signal(
            barrier, inc=1, device_id={"seq": lax.rem(me + d, n)}, device_id_type=MESH
        )

    each(n, greet)

    small[0].wait()
    small[1].wait()
    bk32 = bks[...].astype(F32)
    bv32 = bvs[...].astype(F32)
    for kv in range(KV):
        msg[kv * B : (kv + 1) * B, :] = bk32[:, kv * D : (kv + 1) * D]
        msg[(KV + kv) * B : (KV + kv + 1) * B, :] = bv32[:, kv * D : (kv + 1) * D]
    gat[0] = msg[...].astype(BF16)

    pl.semaphore_wait(barrier, n - 1)

    def gather_copy(d):
        return pltpu.make_async_remote_copy(
            src_ref=gat.at[0],
            dst_ref=gat.at[d],
            send_sem=ag_send,
            recv_sem=ag_recv,
            device_id={"seq": lax.rem(me + d, n)},
            device_id_type=MESH,
        )

    each(n, lambda d: gather_copy(d).start())

    ssf, bcf, fsf = ss[...].astype(F32), bc[...].astype(F32), fs[...].astype(F32)
    col = lax.broadcasted_iota(jnp.int32, (1, n), 1)
    colf = col.astype(F32)
    own_span = jnp.sum(jnp.where(col == me, ssf, 0.0), axis=1, keepdims=True)
    own_first = jnp.sum(jnp.where(colf == own_span, fsf, 0.0), axis=1, keepdims=True)
    own_count = jnp.sum(jnp.where(colf == own_span, bcf, 0.0), axis=1, keepdims=True)
    row = lax.broadcasted_iota(jnp.int32, (rows, n), 0)
    back = me - row // B
    slot = jnp.where(back < 0, back + n, back)
    rcol = lax.broadcasted_iota(jnp.int32, (rows, n), 1)
    key_span = jnp.sum(jnp.where(slot == rcol, ssf, 0.0), axis=1, keepdims=True)
    key_count = jnp.sum(
        jnp.where(rcol.astype(F32) == key_span, bcf, 0.0), axis=1, keepdims=True
    )
    wide_row = lax.broadcasted_iota(jnp.int32, (rows, D), 0)
    wide_lane = lax.broadcasted_iota(jnp.int32, (rows, D), 1)
    beacon = wide_row % B
    live = beacon.astype(F32) < key_count
    earlier = (own_first <= key_span) & (key_span < own_span) & live
    own_beacons = (wide_row < B) & (beacon <= wide_lane % B) & live
    see_raw = jnp.where(earlier, 0.0, LOW)
    see_beacon = jnp.where(earlier | own_beacons, 0.0, LOW)
    causal = lax.broadcasted_iota(jnp.int32, (SPAN, SPAN), 0) <= lax.broadcasted_iota(
        jnp.int32, (SPAN, SPAN), 1
    )
    causal2 = jnp.concatenate([causal] * (CHUNK // SPAN), axis=1)

    for c in small[2:]:
        c.wait()
    bq32 = bqs[...].astype(F32)
    bg32 = jnp.where(
        lax.broadcasted_iota(jnp.int32, (B, 1), 0).astype(F32) < own_count,
        bgs[...].astype(F32),
        0.0,
    )
    for h in range(HEADS):
        qx[h * B : (h + 1) * B, :] = bq32[:, h * D : (h + 1) * D]
        gx[h * B : (h + 1) * B, :] = bg32[:, h * D : (h + 1) * D]
    qxb = qx[...].astype(BF16)
    gxb = gx[...].astype(BF16)
    group_lane = lax.broadcasted_iota(jnp.int32, (1, D), 1) // (GROUP * B)

    def own_keys(kv):
        return k[:, kv * D : (kv + 1) * D], v[:, kv * D : (kv + 1) * D]

    def pick(parts):
        out = parts[0]
        for kv in range(1, KV):
            out = jnp.where(group_lane == kv, parts[kv], out)
        return out

    s = pick([nt(own_keys(kv)[0], qxb) for kv in range(KV)])
    dp = pick([nt(own_keys(kv)[1], gxb) for kv in range(KV)])
    m = jnp.max(s, axis=0, keepdims=True)
    p = jnp.exp2((s - m) * EXP2)
    p_x[...] = p
    dp_x[...] = dp
    x_stat = (m, jnp.sum(p, axis=0, keepdims=True), jnp.sum(p * dp, axis=0, keepdims=True))

    per = CHUNK // SPAN
    for kv in range(KV):
        for c in large[kv]:
            c.wait()
        kr, vr = own_keys(kv)
        for c in range(GROUP // per):
            cols = slice(c * CHUNK, (c + 1) * CHUNK)
            s = nt(kr, stack_heads(q, kv, c * per, per))
            dp = nt(vr, stack_heads(g, kv, c * per, per))
            s = jnp.where(causal2, s, LOW)
            m = jnp.max(s, axis=0, keepdims=True)
            p = jnp.exp2((s - m) * EXP2)
            p_r[kv, :, cols] = p
            dp_r[kv, :, cols] = dp
            stat[kv, 0:1, cols] = m
            stat[kv, 1:2, cols] = jnp.sum(p, axis=0, keepdims=True)
            stat[kv, 2:3, cols] = jnp.sum(p * dp, axis=0, keepdims=True)

    pltpu.make_async_copy(gat.at[pl.ds(1, n - 1)], gat.at[pl.ds(1, n - 1)], ag_recv).wait()
    top = lax.broadcasted_iota(jnp.int32, (1, 8, D), 1) < B
    got = gat[...].astype(F32).reshape(n // 2, 2, 2 * KV * B // 8, 8, D)
    for t in range(2 * KV * B // 8):
        even, odd = got[:, 0, t], got[:, 1, t]
        lo = jnp.where(top, even, pltpu.roll(odd, B, 1))
        hi = jnp.where(top, pltpu.roll(even, B, 1), odd)
        into = kb if t < KV // 2 else vb
        kv = 2 * (t % (KV // 2))
        into[kv] = lo.reshape(rows, D).astype(BF16)
        into[kv + 1] = hi.reshape(rows, D).astype(BF16)

    def beacon_part(s, dp, see, m1, l1, u1):
        s = s + see
        m = jnp.maximum(m1, jnp.max(s, axis=0, keepdims=True))
        p = jnp.exp2((s - m) * EXP2)
        alpha = jnp.exp2((m1 - m) * EXP2)
        total = alpha * l1 + jnp.sum(p, axis=0, keepdims=True)
        inverse = 1.0 / total
        delta = (alpha * u1 + jnp.sum(p * dp, axis=0, keepdims=True)) * inverse
        a = p * inverse
        ds = a * (dp - delta) * SCALE
        return a, ds, alpha * inverse, delta

    a, ds, x_factor, x_delta = beacon_part(
        pick([nt(kb[kv], qxb) for kv in range(KV)]),
        pick([nt(vb[kv], gxb) for kv in range(KV)]),
        see_beacon,
        *x_stat,
    )
    for kv in range(KV):
        a_all[kv, :rows, WIDE:] = jnp.where(group_lane == kv, a, 0.0).astype(BF16)
        ds_all[kv, :rows, WIDE:] = jnp.where(group_lane == kv, ds, 0.0).astype(BF16)
    see2 = jnp.concatenate([see_raw] * per, axis=1)

    def sum_copy(pair, d):
        owner = me - d
        owner = jnp.where(owner < 0, owner + n, owner)
        return pltpu.make_async_remote_copy(
            src_ref=sbuf.at[pair, d],
            dst_ref=rbuf.at[pair, d],
            send_sem=rs_send.at[pair],
            recv_sem=rs_recv.at[pair],
            device_id={"seq": owner},
            device_id_type=MESH,
        )

    for pair in range(KV // 2):
        tiles = []
        for kv in (2 * pair, 2 * pair + 1):
            for c in range(GROUP // per):
                cols = slice(c * CHUNK, (c + 1) * CHUNK)
                a, ds, factor, delta = beacon_part(
                    nt(kb[kv], stack_heads(q, kv, c * per, per)),
                    nt(vb[kv], stack_heads(g, kv, c * per, per)),
                    see2,
                    stat[kv, 0:1, cols],
                    stat[kv, 1:2, cols],
                    stat[kv, 2:3, cols],
                )
                a_all[kv, :rows, cols] = a.astype(BF16)
                ds_all[kv, :rows, cols] = ds.astype(BF16)
                stat[kv, 3:4, cols] = factor
                stat[kv, 4:5, cols] = delta
            q_rows = jnp.concatenate([stack_heads(q, kv, 0, GROUP), qxb], axis=0)
            g_rows = jnp.concatenate([stack_heads(g, kv, 0, GROUP), gxb], axis=0)
            dk = nn(ds_all[kv, :rows, :], q_rows).reshape(n // 2, 8, D)
            dv = nn(a_all[kv, :rows, :], g_rows).reshape(n // 2, 8, D)
            even = jnp.where(top, dk, pltpu.roll(dv, B, 1))
            odd = jnp.where(top, pltpu.roll(dk, B, 1), dv)
            tiles.append(jnp.stack([even, odd], axis=1).reshape(n, 8, D))
        both = jnp.concatenate(tiles, axis=1).astype(BF16)
        sbuf[pair] = both
        rbuf[pair, 0] = both[0]
        each(n, lambda d: sum_copy(pair, d).start())

    out_copies = []
    a = p_x[...] * x_factor
    ds = a * (dp_x[...] - x_delta) * SCALE
    dqx = None
    for kv in range(KV):
        a_all[kv, rows:, WIDE:] = jnp.where(group_lane == kv, a, 0.0).astype(BF16)
        ds_all[kv, rows:, WIDE:] = jnp.where(group_lane == kv, ds, 0.0).astype(BF16)
    for kv in range(KV):
        kr, vr = own_keys(kv)
        keys = jnp.concatenate([kb[kv], kr], axis=0)
        for c in range(GROUP // per):
            cols = slice(c * CHUNK, (c + 1) * CHUNK)
            a = p_r[kv, :, cols] * stat[kv, 3:4, cols]
            ds = a * (dp_r[kv, :, cols] - stat[kv, 4:5, cols]) * SCALE
            a_all[kv, rows:, cols] = a.astype(BF16)
            ds_all[kv, rows:, cols] = ds.astype(BF16)
            dq = tn(ds_all[kv, :, cols], keys).astype(BF16)
            for i in range(per):
                low = (kv * GROUP + c * per + i) * D
                oq[:, low : low + D] = dq[i * SPAN : (i + 1) * SPAN]
        cols = pl.ds(kv * WIDE, WIDE)
        oc = pltpu.make_async_copy(oq.at[:, cols], rq_out.at[:, cols], out_sem.at[kv])
        oc.start()
        out_copies.append(oc)
        term = tn(ds_all[kv, :, WIDE:], keys)
        dqx = term if dqx is None else dqx + term
        q_rows = jnp.concatenate([stack_heads(q, kv, 0, GROUP), qxb], axis=0)
        g_rows = jnp.concatenate([stack_heads(g, kv, 0, GROUP), gxb], axis=0)
        ok[:, kv * D : (kv + 1) * D] = nn(ds_all[kv, rows:, :], q_rows).astype(BF16)
        ov[:, kv * D : (kv + 1) * D] = nn(a_all[kv, rows:, :], g_rows).astype(BF16)
    obq[...] = jnp.concatenate(
        [dqx[h * B : (h + 1) * B] for h in range(HEADS)], axis=1
    ).astype(BF16)
    for i, (a, b) in enumerate([(ok, rk_out), (ov, rv_out), (obq, bq_out)]):
        oc = pltpu.make_async_copy(a, b, out_sem.at[KV + i])
        oc.start()
        out_copies.append(oc)

    dk_parts, dv_parts = [], []
    for pair in range(KV // 2):
        arrived = rbuf.at[pair, pl.ds(1, n - 1)]
        pltpu.make_async_copy(arrived, arrived, rs_recv.at[pair]).wait()
        total = jnp.sum(rbuf[pair].astype(F32), axis=0)
        for i in range(2):
            dk_parts.append(total[8 * i : 8 * i + B])
            dv_parts.append(total[8 * i + B : 8 * i + 8])
    obk[...] = jnp.concatenate(dk_parts, axis=1).astype(BF16)
    obv[...] = jnp.concatenate(dv_parts, axis=1).astype(BF16)
    for i, (a, b) in enumerate([(obk, bk_out), (obv, bv_out)]):
        oc = pltpu.make_async_copy(a, b, out_sem.at[KV + 3 + i])
        oc.start()
        out_copies.append(oc)
    pltpu.make_async_copy(gat.at[pl.ds(1, n - 1)], gat.at[pl.ds(1, n - 1)], ag_send).wait()
    for pair in range(KV // 2):
        left = sbuf.at[pair, pl.ds(1, n - 1)]
        pltpu.make_async_copy(left, left, rs_send.at[pair]).wait()
    for oc in out_copies:
        oc.wait()


def local(n, *args):
    rows = n * B
    keys = rows + SPAN
    rq, bq, rk, rv, bk, bv, rg, bg, ss, bc, fs = args
    out_shape = [jax.ShapeDtypeStruct(x.shape, BF16) for x in (rq, bq, rk, rv, bk, bv)]
    vm = pltpu.VMEM
    any_spec = pl.BlockSpec(memory_space=pl.ANY)
    vmem_spec = pl.BlockSpec(memory_space=pltpu.VMEM)
    scratch = [
        vm(rq.shape, BF16), vm(rg.shape, BF16), vm(rk.shape, BF16), vm(rv.shape, BF16),
        vm(bq.shape, BF16), vm(bg.shape, BF16), vm(bk.shape, BF16), vm(bv.shape, BF16),
        vm((HEADS * B, D), F32), vm((HEADS * B, D), F32),
        vm((2 * KV * B, D), F32), vm((n, 2 * KV * B, D), BF16),
        vm((KV, rows, D), BF16), vm((KV, rows, D), BF16),
        vm((KV, SPAN, WIDE), F32), vm((KV, SPAN, WIDE), F32),
        vm((SPAN, D), F32), vm((SPAN, D), F32), vm((KV, 8, WIDE), F32),
        vm((KV, keys, WIDE + D), BF16), vm((KV, keys, WIDE + D), BF16),
        vm((KV // 2, n, 16, D), BF16), vm((KV // 2, n, 16, D), BF16),
        vm(rq.shape, BF16), vm(bq.shape, BF16), vm(rk.shape, BF16), vm(rv.shape, BF16),
        vm(bk.shape, BF16), vm(bv.shape, BF16),
        pltpu.SemaphoreType.DMA((6 + 2 * KV,)), pltpu.SemaphoreType.DMA((KV + 5,)),
        pltpu.SemaphoreType.DMA, pltpu.SemaphoreType.DMA,
        pltpu.SemaphoreType.DMA((KV // 2,)), pltpu.SemaphoreType.DMA((KV // 2,)),
    ]
    return pl.pallas_call(
        functools.partial(kernel, n),
        out_shape=out_shape,
        in_specs=[any_spec] * 8 + [vmem_spec] * 3,
        out_specs=[any_spec] * 6,
        scratch_shapes=scratch,
        compiler_params=pltpu.CompilerParams(
            collective_id=0, has_side_effects=True, vmem_limit_bytes=50 * 2**20
        ),
    )(rq, bq, rk, rv, bk, bv, rg, bg, ss.reshape(1, n), bc.reshape(1, n), fs.reshape(1, n))


def solution(mesh):
    sharded = P(("grp", "seq"), None)
    return jax.shard_map(
        functools.partial(local, mesh.shape["seq"]),
        mesh=mesh,
        in_specs=(sharded,) * 8 + (P("grp"),) * 3,
        out_specs=(sharded,) * 6,
        check_vma=False,
    )
```

```python
import functools

import jax
import jax.numpy as jnp
from jax import lax
from jax.experimental import pallas as pl
from jax.experimental.pallas import tpu as pltpu
from jax.sharding import PartitionSpec as P

HEADS = 32
KV = 4
D = 128
SPAN = 128
B = 4
GROUP = HEADS // KV
CHUNK = 256
WIDE = GROUP * SPAN
SCALE = D ** (-0.5)
EXP2 = SCALE * 1.4426950408889634
LOW = -1e30
F32 = jnp.float32
BF16 = jnp.bfloat16
VMEM_LIMIT = 48 * 2**20
MESH = pl.DeviceIdType.MESH


def nt(a, b):
    return lax.dot_general(a, b, (((1,), (1,)), ((), ())), preferred_element_type=F32)


def nn(a, b):
    return lax.dot_general(a, b, (((1,), (0,)), ((), ())), preferred_element_type=F32)


def tn(a, b):
    return lax.dot_general(a, b, (((0,), (0,)), ((), ())), preferred_element_type=F32)


def each(n, body):
    if n <= 16:
        for d in range(1, n):
            body(d)
    else:
        lax.fori_loop(1, n, lambda d, c: (body(d), c)[1], 0)


def stack_heads(ref, kv, first, count):
    low = (kv * GROUP + first) * D
    return jnp.concatenate([ref[:, low + i * D : low + (i + 1) * D] for i in range(count)], axis=0)


def kernel(
    n,
    rq, bq, rk, rv, bk, bv, rg, bg, ss, bc, fs,
    oq, obq, ok, ov, obk, obv,
    q, g, k, v, bqs, bgs, bks, bvs, sss, bcs, fss,
    qx, gx, msg, gat, kb, vb,
    p_r, dp_r, p_x, dp_x, stat,
    a_all, ds_all, sbuf, rbuf,
    local_sem, ag_send, ag_recv, rs_send, rs_recv,
):
    me = lax.axis_index("seq")
    rows = n * B

    barrier = pltpu.get_barrier_semaphore()

    def greet(d):
        pl.semaphore_signal(
            barrier, inc=1, device_id={"seq": lax.rem(me + d, n)}, device_id_type=MESH
        )

    each(n, greet)

    pairs = [
        (bk, bks), (bv, bvs), (ss, sss), (bc, bcs), (fs, fss),
        (rk, k), (rv, v), (bq, bqs), (bg, bgs),
    ]
    small = [pltpu.make_async_copy(a, b, local_sem.at[i]) for i, (a, b) in enumerate(pairs)]
    small[0].start()
    small[1].start()

    small[0].wait()
    small[1].wait()
    bk32 = bks[...].astype(F32)
    bv32 = bvs[...].astype(F32)
    for kv in range(KV):
        msg[kv * B : (kv + 1) * B, :] = bk32[:, kv * D : (kv + 1) * D]
        msg[(KV + kv) * B : (KV + kv + 1) * B, :] = bv32[:, kv * D : (kv + 1) * D]
    gat[0] = msg[...].astype(BF16)

    pl.semaphore_wait(barrier, n - 1)

    def gather_copy(d):
        return pltpu.make_async_remote_copy(
            src_ref=gat.at[0],
            dst_ref=gat.at[d],
            send_sem=ag_send,
            recv_sem=ag_recv,
            device_id={"seq": lax.rem(me + d, n)},
            device_id_type=MESH,
        )

    each(n, lambda d: gather_copy(d).start())

    for c in small[2:]:
        c.start()
    large = []
    for kv in range(KV):
        cols = pl.ds(kv * WIDE, WIDE)
        first = len(pairs) + 2 * kv
        cq = pltpu.make_async_copy(rq.at[:, cols], q.at[:, cols], local_sem.at[first])
        cg = pltpu.make_async_copy(rg.at[:, cols], g.at[:, cols], local_sem.at[first + 1])
        cq.start()
        cg.start()
        large.append((cq, cg))
    for c in small[2:]:
        c.wait()

    ssf, bcf, fsf = sss[...].astype(F32), bcs[...].astype(F32), fss[...].astype(F32)
    col = lax.broadcasted_iota(jnp.int32, (1, n), 1)
    colf = col.astype(F32)
    own_span = jnp.sum(jnp.where(col == me, ssf, 0.0), axis=1, keepdims=True)
    own_first = jnp.sum(jnp.where(colf == own_span, fsf, 0.0), axis=1, keepdims=True)
    own_count = jnp.sum(jnp.where(colf == own_span, bcf, 0.0), axis=1, keepdims=True)
    row = lax.broadcasted_iota(jnp.int32, (rows, n), 0)
    back = me - row // B
    slot = jnp.where(back < 0, back + n, back)
    rcol = lax.broadcasted_iota(jnp.int32, (rows, n), 1)
    key_span = jnp.sum(jnp.where(slot == rcol, ssf, 0.0), axis=1, keepdims=True)
    key_count = jnp.sum(
        jnp.where(rcol.astype(F32) == key_span, bcf, 0.0), axis=1, keepdims=True
    )
    wide_row = lax.broadcasted_iota(jnp.int32, (rows, D), 0)
    wide_lane = lax.broadcasted_iota(jnp.int32, (rows, D), 1)
    beacon = wide_row % B
    live = beacon.astype(F32) < key_count
    earlier = (own_first <= key_span) & (key_span < own_span) & live
    own_beacons = (wide_row < B) & (beacon <= wide_lane % B) & live
    see_raw = jnp.where(earlier, 0.0, LOW)
    see_beacon = jnp.where(earlier | own_beacons, 0.0, LOW)
    causal = lax.broadcasted_iota(jnp.int32, (SPAN, SPAN), 0) <= lax.broadcasted_iota(
        jnp.int32, (SPAN, SPAN), 1
    )
    causal2 = jnp.concatenate([causal] * (CHUNK // SPAN), axis=1)

    bq32 = bqs[...].astype(F32)
    bg32 = jnp.where(
        lax.broadcasted_iota(jnp.int32, (B, 1), 0).astype(F32) < own_count,
        bgs[...].astype(F32),
        0.0,
    )
    for h in range(HEADS):
        qx[h * B : (h + 1) * B, :] = bq32[:, h * D : (h + 1) * D]
        gx[h * B : (h + 1) * B, :] = bg32[:, h * D : (h + 1) * D]
    qxb = qx[...].astype(BF16)
    gxb = gx[...].astype(BF16)
    group_lane = lax.broadcasted_iota(jnp.int32, (1, D), 1) // (GROUP * B)

    def own_keys(kv):
        return k[:, kv * D : (kv + 1) * D], v[:, kv * D : (kv + 1) * D]

    def pick(parts):
        out = parts[0]
        for kv in range(1, KV):
            out = jnp.where(group_lane == kv, parts[kv], out)
        return out

    s = pick([nt(own_keys(kv)[0], qxb) for kv in range(KV)])
    dp = pick([nt(own_keys(kv)[1], gxb) for kv in range(KV)])
    m = jnp.max(s, axis=0, keepdims=True)
    p = jnp.exp2((s - m) * EXP2)
    p_x[...] = p
    dp_x[...] = dp
    x_stat = (m, jnp.sum(p, axis=0, keepdims=True), jnp.sum(p * dp, axis=0, keepdims=True))

    per = CHUNK // SPAN
    for kv in range(KV):
        for c in large[kv]:
            c.wait()
        kr, vr = own_keys(kv)
        for c in range(GROUP // per):
            cols = slice(c * CHUNK, (c + 1) * CHUNK)
            s = nt(kr, stack_heads(q, kv, c * per, per))
            dp = nt(vr, stack_heads(g, kv, c * per, per))
            s = jnp.where(causal2, s, LOW)
            m = jnp.max(s, axis=0, keepdims=True)
            p = jnp.exp2((s - m) * EXP2)
            p_r[kv, :, cols] = p
            dp_r[kv, :, cols] = dp
            stat[kv, 0:1, cols] = m
            stat[kv, 1:2, cols] = jnp.sum(p, axis=0, keepdims=True)
            stat[kv, 2:3, cols] = jnp.sum(p * dp, axis=0, keepdims=True)

    pltpu.make_async_copy(gat.at[pl.ds(1, n - 1)], gat.at[pl.ds(1, n - 1)], ag_recv).wait()
    top = lax.broadcasted_iota(jnp.int32, (1, 8, D), 1) < B
    got = gat[...].astype(F32).reshape(n // 2, 2, 2 * KV * B // 8, 8, D)
    for t in range(2 * KV * B // 8):
        even, odd = got[:, 0, t], got[:, 1, t]
        lo = jnp.where(top, even, pltpu.roll(odd, B, 1))
        hi = jnp.where(top, pltpu.roll(even, B, 1), odd)
        into = kb if t < KV // 2 else vb
        kv = 2 * (t % (KV // 2))
        into[kv] = lo.reshape(rows, D).astype(BF16)
        into[kv + 1] = hi.reshape(rows, D).astype(BF16)

    def beacon_part(s, dp, see, m1, l1, u1):
        s = s + see
        m = jnp.maximum(m1, jnp.max(s, axis=0, keepdims=True))
        p = jnp.exp2((s - m) * EXP2)
        alpha = jnp.exp2((m1 - m) * EXP2)
        total = alpha * l1 + jnp.sum(p, axis=0, keepdims=True)
        inverse = 1.0 / total
        delta = (alpha * u1 + jnp.sum(p * dp, axis=0, keepdims=True)) * inverse
        a = p * inverse
        ds = a * (dp - delta) * SCALE
        return a, ds, alpha * inverse, delta

    a, ds, x_factor, x_delta = beacon_part(
        pick([nt(kb[kv], qxb) for kv in range(KV)]),
        pick([nt(vb[kv], gxb) for kv in range(KV)]),
        see_beacon,
        *x_stat,
    )
    for kv in range(KV):
        a_all[kv, :rows, WIDE:] = jnp.where(group_lane == kv, a, 0.0).astype(BF16)
        ds_all[kv, :rows, WIDE:] = jnp.where(group_lane == kv, ds, 0.0).astype(BF16)
    see2 = jnp.concatenate([see_raw] * per, axis=1)

    def sum_copy(pair, d):
        owner = me - d
        owner = jnp.where(owner < 0, owner + n, owner)
        return pltpu.make_async_remote_copy(
            src_ref=sbuf.at[pair, d],
            dst_ref=rbuf.at[pair, d],
            send_sem=rs_send.at[pair],
            recv_sem=rs_recv.at[pair],
            device_id={"seq": owner},
            device_id_type=MESH,
        )

    for pair in range(KV // 2):
        tiles = []
        for kv in (2 * pair, 2 * pair + 1):
            for c in range(GROUP // per):
                cols = slice(c * CHUNK, (c + 1) * CHUNK)
                a, ds, factor, delta = beacon_part(
                    nt(kb[kv], stack_heads(q, kv, c * per, per)),
                    nt(vb[kv], stack_heads(g, kv, c * per, per)),
                    see2,
                    stat[kv, 0:1, cols],
                    stat[kv, 1:2, cols],
                    stat[kv, 2:3, cols],
                )
                a_all[kv, :rows, cols] = a.astype(BF16)
                ds_all[kv, :rows, cols] = ds.astype(BF16)
                stat[kv, 3:4, cols] = factor
                stat[kv, 4:5, cols] = delta
            q_rows = jnp.concatenate([stack_heads(q, kv, 0, GROUP), qxb], axis=0)
            g_rows = jnp.concatenate([stack_heads(g, kv, 0, GROUP), gxb], axis=0)
            dk = nn(ds_all[kv, :rows, :], q_rows).reshape(n // 2, 8, D)
            dv = nn(a_all[kv, :rows, :], g_rows).reshape(n // 2, 8, D)
            even = jnp.where(top, dk, pltpu.roll(dv, B, 1))
            odd = jnp.where(top, pltpu.roll(dk, B, 1), dv)
            tiles.append(jnp.stack([even, odd], axis=1).reshape(n, 8, D))
        both = jnp.concatenate(tiles, axis=1).astype(BF16)
        sbuf[pair] = both
        rbuf[pair, 0] = both[0]
        each(n, lambda d: sum_copy(pair, d).start())

    a = p_x[...] * x_factor
    ds = a * (dp_x[...] - x_delta) * SCALE
    dqx = None
    for kv in range(KV):
        a_all[kv, rows:, WIDE:] = jnp.where(group_lane == kv, a, 0.0).astype(BF16)
        ds_all[kv, rows:, WIDE:] = jnp.where(group_lane == kv, ds, 0.0).astype(BF16)
    for kv in range(KV):
        kr, vr = own_keys(kv)
        keys = jnp.concatenate([kb[kv], kr], axis=0)
        for c in range(GROUP // per):
            cols = slice(c * CHUNK, (c + 1) * CHUNK)
            a = p_r[kv, :, cols] * stat[kv, 3:4, cols]
            ds = a * (dp_r[kv, :, cols] - stat[kv, 4:5, cols]) * SCALE
            a_all[kv, rows:, cols] = a.astype(BF16)
            ds_all[kv, rows:, cols] = ds.astype(BF16)
            dq = tn(ds_all[kv, :, cols], keys).astype(BF16)
            for i in range(per):
                low = (kv * GROUP + c * per + i) * D
                oq[:, low : low + D] = dq[i * SPAN : (i + 1) * SPAN]
        term = tn(ds_all[kv, :, WIDE:], keys)
        dqx = term if dqx is None else dqx + term
        q_rows = jnp.concatenate([stack_heads(q, kv, 0, GROUP), qxb], axis=0)
        g_rows = jnp.concatenate([stack_heads(g, kv, 0, GROUP), gxb], axis=0)
        ok[:, kv * D : (kv + 1) * D] = nn(ds_all[kv, rows:, :], q_rows).astype(BF16)
        ov[:, kv * D : (kv + 1) * D] = nn(a_all[kv, rows:, :], g_rows).astype(BF16)
    obq[...] = jnp.concatenate(
        [dqx[h * B : (h + 1) * B] for h in range(HEADS)], axis=1
    ).astype(BF16)

    dk_parts, dv_parts = [], []
    for pair in range(KV // 2):
        arrived = rbuf.at[pair, pl.ds(1, n - 1)]
        pltpu.make_async_copy(arrived, arrived, rs_recv.at[pair]).wait()
        total = jnp.sum(rbuf[pair].astype(F32), axis=0)
        for i in range(2):
            dk_parts.append(total[8 * i : 8 * i + B])
            dv_parts.append(total[8 * i + B : 8 * i + 8])
    obk[...] = jnp.concatenate(dk_parts, axis=1).astype(BF16)
    obv[...] = jnp.concatenate(dv_parts, axis=1).astype(BF16)
    pltpu.make_async_copy(gat.at[pl.ds(1, n - 1)], gat.at[pl.ds(1, n - 1)], ag_send).wait()
    for pair in range(KV // 2):
        left = sbuf.at[pair, pl.ds(1, n - 1)]
        pltpu.make_async_copy(left, left, rs_send.at[pair]).wait()


def hand_out(*refs):
    sem = refs[12]
    copies = [pltpu.make_async_copy(refs[i], refs[6 + i], sem.at[i]) for i in range(6)]
    for c in copies:
        c.start()
    for c in copies:
        c.wait()


def local(n, *args):
    rows = n * B
    keys = rows + SPAN
    rq, bq, rk, rv, bk, bv, rg, bg, ss, bc, fs = args
    out_shape = [jax.ShapeDtypeStruct(x.shape, BF16) for x in (rq, bq, rk, rv, bk, bv)]
    vm = pltpu.VMEM
    any_spec = pl.BlockSpec(memory_space=pl.ANY)
    hbm_spec = pl.BlockSpec(memory_space=pltpu.HBM)
    vmem_spec = pl.BlockSpec(memory_space=pltpu.VMEM)
    scratch = [
        vm(rq.shape, BF16), vm(rg.shape, BF16), vm(rk.shape, BF16), vm(rv.shape, BF16),
        vm(bq.shape, BF16), vm(bg.shape, BF16), vm(bk.shape, BF16), vm(bv.shape, BF16),
        vm((1, n), jnp.int32), vm((1, n), jnp.int32), vm((1, n), jnp.int32),
        vm((HEADS * B, D), F32), vm((HEADS * B, D), F32),
        vm((2 * KV * B, D), F32), vm((n, 2 * KV * B, D), BF16),
        vm((KV, rows, D), BF16), vm((KV, rows, D), BF16),
        vm((KV, SPAN, WIDE), F32), vm((KV, SPAN, WIDE), F32),
        vm((SPAN, D), F32), vm((SPAN, D), F32), vm((KV, 8, WIDE), F32),
        vm((KV, keys, WIDE + D), BF16), vm((KV, keys, WIDE + D), BF16),
        vm((KV // 2, n, 16, D), BF16), vm((KV // 2, n, 16, D), BF16),
        pltpu.SemaphoreType.DMA((9 + 2 * KV,)),
        pltpu.SemaphoreType.DMA, pltpu.SemaphoreType.DMA,
        pltpu.SemaphoreType.DMA((KV // 2,)), pltpu.SemaphoreType.DMA((KV // 2,)),
    ]
    ins = [rq, bq, rk, rv, bk, bv, rg, bg] + [x.reshape(1, n) for x in (ss, bc, fs)]
    made = pl.pallas_call(
        functools.partial(kernel, n),
        out_shape=[pltpu.VMEM(x.shape, BF16) for x in out_shape],
        in_specs=[hbm_spec] * 11,
        out_specs=[vmem_spec] * 6,
        scratch_shapes=scratch,
        compiler_params=pltpu.CompilerParams(
            collective_id=0, has_side_effects=True, vmem_limit_bytes=VMEM_LIMIT
        ),
    )(*[pltpu.with_memory_space_constraint(x, pltpu.HBM) for x in ins])
    return pl.pallas_call(
        hand_out,
        out_shape=[pltpu.HBM(x.shape, BF16) for x in out_shape],
        in_specs=[any_spec] * 6,
        out_specs=[hbm_spec] * 6,
        scratch_shapes=[pltpu.SemaphoreType.DMA((6,))],
        compiler_params=pltpu.CompilerParams(vmem_limit_bytes=2**20),
    )(*made)


def solution(mesh):
    sharded = P(("grp", "seq"), None)
    return jax.shard_map(
        functools.partial(local, mesh.shape["seq"]),
        mesh=mesh,
        in_specs=(sharded,) * 8 + (P("grp"),) * 3,
        out_specs=(sharded,) * 6,
        check_vma=False,
    )
```

```python
import functools

import jax
import jax.numpy as jnp
from jax import lax
from jax.experimental import pallas as pl
from jax.experimental.pallas import tpu as pltpu
from jax.sharding import PartitionSpec as P

HEADS = 32
KV = 4
D = 128
SPAN = 128
B = 4
GROUP = HEADS // KV
CHUNK = 256
WIDE = GROUP * SPAN
SCALE = D ** (-0.5)
EXP2 = SCALE * 1.4426950408889634
LOW = -1e30
F32 = jnp.float32
BF16 = jnp.bfloat16
VMEM_LIMIT = 48 * 2**20
MESH = pl.DeviceIdType.MESH


def nt(a, b):
    return lax.dot_general(a, b, (((1,), (1,)), ((), ())), preferred_element_type=F32)


def nn(a, b):
    return lax.dot_general(a, b, (((1,), (0,)), ((), ())), preferred_element_type=F32)


def tn(a, b):
    return lax.dot_general(a, b, (((0,), (0,)), ((), ())), preferred_element_type=F32)


def each(n, body):
    if n <= 16:
        for d in range(1, n):
            body(d)
    else:
        lax.fori_loop(1, n, lambda d, c: (body(d), c)[1], 0)


def stack_heads(ref, kv, first, count):
    low = (kv * GROUP + first) * D
    return jnp.concatenate([ref[:, low + i * D : low + (i + 1) * D] for i in range(count)], axis=0)


def kernel(
    n,
    rq, bq, rk, rv, bk, bv, rg, bg, ss, bc, fs,
    oq, obq, ok, ov, obk, obv,
    q, g, k, v, bqs, bgs, bks, bvs, sss, bcs, fss,
    qx, gx, msg, gat, kb, vb,
    p_r, dp_r, p_x, dp_x, stat,
    a_all, ds_all, sbuf, rbuf,
    local_sem, ag_send, ag_recv, rs_send, rs_recv,
):
    me = lax.axis_index("seq")
    rows = n * B

    def ahead(d):
        return jnp.where(me + d >= n, me + d - n, me + d)

    barrier = pltpu.get_barrier_semaphore()

    def greet(d):
        pl.semaphore_signal(
            barrier, inc=1, device_id={"seq": ahead(d)}, device_id_type=MESH
        )

    each(n, greet)

    pairs = [
        (bk, bks), (bv, bvs), (ss, sss), (bc, bcs), (fs, fss),
        (rk, k), (rv, v), (bq, bqs), (bg, bgs),
    ]
    small = [pltpu.make_async_copy(a, b, local_sem.at[i]) for i, (a, b) in enumerate(pairs)]
    small[0].start()
    small[1].start()

    for c in small[2:]:
        c.start()
    large = []
    for kv in range(KV):
        cols = pl.ds(kv * WIDE, WIDE)
        first = len(pairs) + 2 * kv
        cq = pltpu.make_async_copy(rq.at[:, cols], q.at[:, cols], local_sem.at[first])
        cg = pltpu.make_async_copy(rg.at[:, cols], g.at[:, cols], local_sem.at[first + 1])
        cq.start()
        cg.start()
        large.append((cq, cg))

    small[0].wait()
    small[1].wait()
    bk32 = bks[...].astype(F32)
    bv32 = bvs[...].astype(F32)
    for kv in range(KV):
        msg[kv * B : (kv + 1) * B, :] = bk32[:, kv * D : (kv + 1) * D]
        msg[(KV + kv) * B : (KV + kv + 1) * B, :] = bv32[:, kv * D : (kv + 1) * D]
    gat[0] = msg[...].astype(BF16)

    pl.semaphore_wait(barrier, n - 1)

    def gather_copy(d):
        return pltpu.make_async_remote_copy(
            src_ref=gat.at[0],
            dst_ref=gat.at[d],
            send_sem=ag_send,
            recv_sem=ag_recv,
            device_id={"seq": ahead(d)},
            device_id_type=MESH,
        )

    each(n, lambda d: gather_copy(d).start())

    for c in small[2:]:
        c.wait()

    ssf, bcf, fsf = sss[...].astype(F32), bcs[...].astype(F32), fss[...].astype(F32)
    col = lax.broadcasted_iota(jnp.int32, (1, n), 1)
    colf = col.astype(F32)
    own_span = jnp.sum(jnp.where(col == me, ssf, 0.0), axis=1, keepdims=True)
    own_first = jnp.sum(jnp.where(colf == own_span, fsf, 0.0), axis=1, keepdims=True)
    own_count = jnp.sum(jnp.where(colf == own_span, bcf, 0.0), axis=1, keepdims=True)
    row = lax.broadcasted_iota(jnp.int32, (rows, n), 0)
    back = me - row // B
    slot = jnp.where(back < 0, back + n, back)
    rcol = lax.broadcasted_iota(jnp.int32, (rows, n), 1)
    key_span = jnp.sum(jnp.where(slot == rcol, ssf, 0.0), axis=1, keepdims=True)
    key_count = jnp.sum(
        jnp.where(rcol.astype(F32) == key_span, bcf, 0.0), axis=1, keepdims=True
    )
    wide_row = lax.broadcasted_iota(jnp.int32, (rows, D), 0)
    wide_lane = lax.broadcasted_iota(jnp.int32, (rows, D), 1)
    beacon = wide_row % B
    live = beacon.astype(F32) < key_count
    earlier = (own_first <= key_span) & (key_span < own_span) & live
    own_beacons = (wide_row < B) & (beacon <= wide_lane % B) & live
    see_raw = jnp.where(earlier, 0.0, LOW)
    see_beacon = jnp.where(earlier | own_beacons, 0.0, LOW)
    causal = lax.broadcasted_iota(jnp.int32, (SPAN, SPAN), 0) <= lax.broadcasted_iota(
        jnp.int32, (SPAN, SPAN), 1
    )
    causal2 = jnp.concatenate([causal] * (CHUNK // SPAN), axis=1)

    bq32 = bqs[...].astype(F32)
    bg32 = jnp.where(
        lax.broadcasted_iota(jnp.int32, (B, 1), 0).astype(F32) < own_count,
        bgs[...].astype(F32),
        0.0,
    )
    for h in range(HEADS):
        qx[h * B : (h + 1) * B, :] = bq32[:, h * D : (h + 1) * D]
        gx[h * B : (h + 1) * B, :] = bg32[:, h * D : (h + 1) * D]
    qxb = qx[...].astype(BF16)
    gxb = gx[...].astype(BF16)
    group_lane = lax.broadcasted_iota(jnp.int32, (1, D), 1) // (GROUP * B)

    def own_keys(kv):
        return k[:, kv * D : (kv + 1) * D], v[:, kv * D : (kv + 1) * D]

    def pick(parts):
        out = parts[0]
        for kv in range(1, KV):
            out = jnp.where(group_lane == kv, parts[kv], out)
        return out

    s = pick([nt(own_keys(kv)[0], qxb) for kv in range(KV)])
    dp = pick([nt(own_keys(kv)[1], gxb) for kv in range(KV)])
    m = jnp.max(s, axis=0, keepdims=True)
    p = jnp.exp2((s - m) * EXP2)
    p_x[...] = p
    dp_x[...] = dp
    x_stat = (m, jnp.sum(p, axis=0, keepdims=True), jnp.sum(p * dp, axis=0, keepdims=True))

    per = CHUNK // SPAN
    for kv in range(KV):
        for c in large[kv]:
            c.wait()
        kr, vr = own_keys(kv)
        for c in range(GROUP // per):
            cols = slice(c * CHUNK, (c + 1) * CHUNK)
            s = nt(kr, stack_heads(q, kv, c * per, per))
            dp = nt(vr, stack_heads(g, kv, c * per, per))
            s = jnp.where(causal2, s, LOW)
            m = jnp.max(s, axis=0, keepdims=True)
            p = jnp.exp2((s - m) * EXP2)
            p_r[kv, :, cols] = p
            dp_r[kv, :, cols] = dp
            stat[kv, 0:1, cols] = m
            stat[kv, 1:2, cols] = jnp.sum(p, axis=0, keepdims=True)
            stat[kv, 2:3, cols] = jnp.sum(p * dp, axis=0, keepdims=True)

    pltpu.make_async_copy(gat.at[pl.ds(1, n - 1)], gat.at[pl.ds(1, n - 1)], ag_recv).wait()
    top = lax.broadcasted_iota(jnp.int32, (1, 8, D), 1) < B
    got = gat[...].astype(F32).reshape(n // 2, 2, 2 * KV * B // 8, 8, D)
    for t in range(2 * KV * B // 8):
        even, odd = got[:, 0, t], got[:, 1, t]
        lo = jnp.where(top, even, pltpu.roll(odd, B, 1))
        hi = jnp.where(top, pltpu.roll(even, B, 1), odd)
        into = kb if t < KV // 2 else vb
        kv = 2 * (t % (KV // 2))
        into[kv] = lo.reshape(rows, D).astype(BF16)
        into[kv + 1] = hi.reshape(rows, D).astype(BF16)

    def beacon_part(s, dp, see, m1, l1, u1):
        s = s + see
        m = jnp.maximum(m1, jnp.max(s, axis=0, keepdims=True))
        p = jnp.exp2((s - m) * EXP2)
        alpha = jnp.exp2((m1 - m) * EXP2)
        total = alpha * l1 + jnp.sum(p, axis=0, keepdims=True)
        inverse = 1.0 / total
        delta = (alpha * u1 + jnp.sum(p * dp, axis=0, keepdims=True)) * inverse
        a = p * inverse
        ds = a * (dp - delta) * SCALE
        return a, ds, alpha * inverse, delta

    a, ds, x_factor, x_delta = beacon_part(
        pick([nt(kb[kv], qxb) for kv in range(KV)]),
        pick([nt(vb[kv], gxb) for kv in range(KV)]),
        see_beacon,
        *x_stat,
    )
    for kv in range(KV):
        a_all[kv, :rows, WIDE:] = jnp.where(group_lane == kv, a, 0.0).astype(BF16)
        ds_all[kv, :rows, WIDE:] = jnp.where(group_lane == kv, ds, 0.0).astype(BF16)
    see2 = jnp.concatenate([see_raw] * per, axis=1)

    def sum_copy(pair, d):
        owner = me - d
        owner = jnp.where(owner < 0, owner + n, owner)
        return pltpu.make_async_remote_copy(
            src_ref=sbuf.at[pair, d],
            dst_ref=rbuf.at[pair, d],
            send_sem=rs_send.at[pair],
            recv_sem=rs_recv.at[pair],
            device_id={"seq": owner},
            device_id_type=MESH,
        )

    for pair in range(KV // 2):
        tiles = []
        for kv in (2 * pair, 2 * pair + 1):
            for c in range(GROUP // per):
                cols = slice(c * CHUNK, (c + 1) * CHUNK)
                a, ds, factor, delta = beacon_part(
                    nt(kb[kv], stack_heads(q, kv, c * per, per)),
                    nt(vb[kv], stack_heads(g, kv, c * per, per)),
                    see2,
                    stat[kv, 0:1, cols],
                    stat[kv, 1:2, cols],
                    stat[kv, 2:3, cols],
                )
                a_all[kv, :rows, cols] = a.astype(BF16)
                ds_all[kv, :rows, cols] = ds.astype(BF16)
                stat[kv, 3:4, cols] = factor
                stat[kv, 4:5, cols] = delta
            q_rows = jnp.concatenate([stack_heads(q, kv, 0, GROUP), qxb], axis=0)
            g_rows = jnp.concatenate([stack_heads(g, kv, 0, GROUP), gxb], axis=0)
            dk = nn(ds_all[kv, :rows, :], q_rows).reshape(n // 2, 8, D)
            dv = nn(a_all[kv, :rows, :], g_rows).reshape(n // 2, 8, D)
            even = jnp.where(top, dk, pltpu.roll(dv, B, 1))
            odd = jnp.where(top, pltpu.roll(dk, B, 1), dv)
            tiles.append(jnp.stack([even, odd], axis=1).reshape(n, 8, D))
        both = jnp.concatenate(tiles, axis=1).astype(BF16)
        sbuf[pair] = both
        rbuf[pair, 0] = both[0]
        each(n, lambda d: sum_copy(pair, d).start())

    a = p_x[...] * x_factor
    ds = a * (dp_x[...] - x_delta) * SCALE
    dqx = None
    for kv in range(KV):
        a_all[kv, rows:, WIDE:] = jnp.where(group_lane == kv, a, 0.0).astype(BF16)
        ds_all[kv, rows:, WIDE:] = jnp.where(group_lane == kv, ds, 0.0).astype(BF16)
    for kv in range(KV):
        kr, vr = own_keys(kv)
        keys = jnp.concatenate([kb[kv], kr], axis=0)
        for c in range(GROUP // per):
            cols = slice(c * CHUNK, (c + 1) * CHUNK)
            a = p_r[kv, :, cols] * stat[kv, 3:4, cols]
            ds = a * (dp_r[kv, :, cols] - stat[kv, 4:5, cols]) * SCALE
            a_all[kv, rows:, cols] = a.astype(BF16)
            ds_all[kv, rows:, cols] = ds.astype(BF16)
            dq = tn(ds_all[kv, :, cols], keys).astype(BF16)
            for i in range(per):
                low = (kv * GROUP + c * per + i) * D
                oq[:, low : low + D] = dq[i * SPAN : (i + 1) * SPAN]
        term = tn(ds_all[kv, :, WIDE:], keys)
        dqx = term if dqx is None else dqx + term
        q_rows = jnp.concatenate([stack_heads(q, kv, 0, GROUP), qxb], axis=0)
        g_rows = jnp.concatenate([stack_heads(g, kv, 0, GROUP), gxb], axis=0)
        ok[:, kv * D : (kv + 1) * D] = nn(ds_all[kv, rows:, :], q_rows).astype(BF16)
        ov[:, kv * D : (kv + 1) * D] = nn(a_all[kv, rows:, :], g_rows).astype(BF16)
    obq[...] = jnp.concatenate(
        [dqx[h * B : (h + 1) * B] for h in range(HEADS)], axis=1
    ).astype(BF16)

    dk_parts, dv_parts = [], []
    for pair in range(KV // 2):
        arrived = rbuf.at[pair, pl.ds(1, n - 1)]
        pltpu.make_async_copy(arrived, arrived, rs_recv.at[pair]).wait()
        total = jnp.sum(rbuf[pair].astype(F32), axis=0)
        for i in range(2):
            dk_parts.append(total[8 * i : 8 * i + B])
            dv_parts.append(total[8 * i + B : 8 * i + 8])
    obk[...] = jnp.concatenate(dk_parts, axis=1).astype(BF16)
    obv[...] = jnp.concatenate(dv_parts, axis=1).astype(BF16)
    pltpu.make_async_copy(gat.at[pl.ds(1, n - 1)], gat.at[pl.ds(1, n - 1)], ag_send).wait()
    for pair in range(KV // 2):
        left = sbuf.at[pair, pl.ds(1, n - 1)]
        pltpu.make_async_copy(left, left, rs_send.at[pair]).wait()


def hand_out(*refs):
    sem = refs[12]
    copies = [pltpu.make_async_copy(refs[i], refs[6 + i], sem.at[i]) for i in range(1, 6)]
    for i in range(4):
        part = pl.ds(i * SPAN // 4, SPAN // 4)
        copies.append(
            pltpu.make_async_copy(refs[0].at[part], refs[6].at[part], sem.at[(0, 6, 7, 8)[i]])
        )
    for c in copies:
        c.start()
    for c in copies:
        c.wait()


def local(n, *args):
    rows = n * B
    keys = rows + SPAN
    rq, bq, rk, rv, bk, bv, rg, bg, ss, bc, fs = args
    out_shape = [jax.ShapeDtypeStruct(x.shape, BF16) for x in (rq, bq, rk, rv, bk, bv)]
    vm = pltpu.VMEM
    any_spec = pl.BlockSpec(memory_space=pl.ANY)
    hbm_spec = pl.BlockSpec(memory_space=pltpu.HBM)
    vmem_spec = pl.BlockSpec(memory_space=pltpu.VMEM)
    scratch = [
        vm(rq.shape, BF16), vm(rg.shape, BF16), vm(rk.shape, BF16), vm(rv.shape, BF16),
        vm(bq.shape, BF16), vm(bg.shape, BF16), vm(bk.shape, BF16), vm(bv.shape, BF16),
        vm((1, n), jnp.int32), vm((1, n), jnp.int32), vm((1, n), jnp.int32),
        vm((HEADS * B, D), F32), vm((HEADS * B, D), F32),
        vm((2 * KV * B, D), F32), vm((n, 2 * KV * B, D), BF16),
        vm((KV, rows, D), BF16), vm((KV, rows, D), BF16),
        vm((KV, SPAN, WIDE), F32), vm((KV, SPAN, WIDE), F32),
        vm((SPAN, D), F32), vm((SPAN, D), F32), vm((KV, 8, WIDE), F32),
        vm((KV, keys, WIDE + D), BF16), vm((KV, keys, WIDE + D), BF16),
        vm((KV // 2, n, 16, D), BF16), vm((KV // 2, n, 16, D), BF16),
        pltpu.SemaphoreType.DMA((9 + 2 * KV,)),
        pltpu.SemaphoreType.DMA, pltpu.SemaphoreType.DMA,
        pltpu.SemaphoreType.DMA((KV // 2,)), pltpu.SemaphoreType.DMA((KV // 2,)),
    ]
    ins = [rq, bq, rk, rv, bk, bv, rg, bg] + [x.reshape(1, n) for x in (ss, bc, fs)]
    made = pl.pallas_call(
        functools.partial(kernel, n),
        out_shape=[pltpu.VMEM(x.shape, BF16) for x in out_shape],
        in_specs=[hbm_spec] * 11,
        out_specs=[vmem_spec] * 6,
        scratch_shapes=scratch,
        compiler_params=pltpu.CompilerParams(
            collective_id=0, has_side_effects=True, vmem_limit_bytes=VMEM_LIMIT
        ),
    )(*[pltpu.with_memory_space_constraint(x, pltpu.HBM) for x in ins])
    return pl.pallas_call(
        hand_out,
        out_shape=[pltpu.HBM(x.shape, BF16) for x in out_shape],
        in_specs=[any_spec] * 6,
        out_specs=[hbm_spec] * 6,
        scratch_shapes=[pltpu.SemaphoreType.DMA((9,))],
        compiler_params=pltpu.CompilerParams(vmem_limit_bytes=2**20),
    )(*made)


def solution(mesh):
    sharded = P(("grp", "seq"), None)
    return jax.shard_map(
        functools.partial(local, mesh.shape["seq"]),
        mesh=mesh,
        in_specs=(sharded,) * 8 + (P("grp"),) * 3,
        out_specs=(sharded,) * 6,
        check_vma=False,
    )
```
